512 devices in a mesh: row: 16 (over z), space: 32 (over y, x, core).
Axes of the slice: x: 4, y: 4, z: 16, core: 2. Of those that a mesh axis runs over, the one named last changes fastest.
Arguments:
- features: bfloat16 [8192, 128], P(('row', 'space')), may hold values from -6 to 6
- positions: float32 [3, 8192], P(None, ('row', 'space')), may hold values from -0.5 to 78, as said below
- species: int32 [8192], P(('row', 'space')), may hold values from 0 to 3
- ghost_list: int32 [16, 1024, 32], P('row', 'space'), may hold values from 0 to 15
- edge_recv: int32 [262144], P(('row', 'space')), may hold values from 0 to 16, as said below
- edge_send: int32 [262144], P(('row', 'space')), may hold values from 0 to 1039
- edge_vec: float32 [3, 262144], P(None, ('row', 'space')), may hold values from -5.8 to 5.8, as said below
- w_msg: bfloat16 [128, 256], replicated, may hold values from -0.5 to 0.5
- w_rad1: float32 [8, 128], replicated, may hold values from -2 to 2
- w_rad2: bfloat16 [128, 256], replicated, may hold values from -0.5 to 0.5
- w_up: bfloat16 [256, 128], replicated, may hold values from -0.375 to 0.375
- w_out: float32 [128], replicated, may hold values from -0.5 to 0.5
- hardness: float32 [4], replicated, may hold values from 2 to 4
- width: float32 [4], replicated, may hold values from 0.8 to 1.6
- chi_shift: float32 [4], replicated, may hold values from -1 to 1
- field: float32 [1], replicated, may hold values from 0.01 to 0.03
Outputs:
- new_features: bfloat16 [8192, 128], P(('row', 'space'))
- charges: float32 [8192], P(('row', 'space'))
- forces: float32 [3, 8192], P(None, ('row', 'space'))
- virial: float32 [6, 8192], P(None, ('row', 'space'))
The draws below stay inside these ranges and needn't reach their ends.
Inputs may be any that keep to these rules, and one draw needn't show every extreme that they name: `edge_recv`: in every domain the edges are ordered by receiver; the slots in use fill the first whole blocks of 128 rows, a quarter of the blocks or more, and the other slots hold 16; some domain uses all its slots. `positions`: every two atoms are 1.5 or more apart. `edge_vec`: each edge's length lies between 1.2 and 5.8.
All inputs are finite; a program needn't handle non-finite values.
Results may differ from the reference program's by a relative error of at most 0.0045.
Values may be sent and summed in bfloat16 or wider, within the bound.
A program may use at most 64 MiB of HBM per device.

```python
import math
import jax
import jax.numpy as jnp
from jax import lax

ATOM_DEV = 16
CH = 128
CAP = 32
EBLK = 128
NRBF = 8
NSPEC = 4
ITERS = 2
ATOMS = 8192
EDGE_DEV = 512
EDGES = 262144
N_ROW = 16
N_SPACE = 32


def draw_positions(key, part):
    index = jnp.arange(ATOMS, dtype=jnp.int32)
    domain = index // ATOM_DEV
    local = index % ATOM_DEV
    group = domain // N_SPACE
    lane = domain % N_SPACE
    layers = ATOM_DEV // 16
    first_cell = lane // 4 * 4 + local % 4
    second_cell = lane % 4 * 4 + local // 4 % 4
    third_cell = group * layers + local // 16
    lattice = jnp.stack([first_cell, second_cell, third_cell]).astype(jnp.float32) * 2.5
    jitter = jnp.clip(0.2 * jax.random.normal(key, (3, ATOMS), jnp.float32), -0.5, 0.5)
    return lattice + jitter


def draw_edge_vec(key, part):
    first_key, second_key = jax.random.split(key)
    heading = jax.random.normal(first_key, (3, EDGES), jnp.float32)
    heading = heading / jnp.sqrt(jnp.sum(heading * heading, axis=0) + 1e-06)
    length = jax.random.uniform(second_key, (EDGES,), jnp.float32, 1.2, 5.8)
    return heading * length[None, :]


def draw_edge_recv(key, part):
    domains = EDGES // EDGE_DEV
    blocks = EDGE_DEV // EBLK
    lowest = max(1, blocks // 4)
    first_key, second_key, third_key, fourth_key = jax.random.split(key, 4)
    one_draw = jax.random.randint(first_key, (domains,), lowest, blocks + 1)
    other_draw = jax.random.randint(second_key, (domains,), lowest, blocks + 1)
    live = jnp.minimum(one_draw, other_draw)
    order = jax.random.permutation(third_key, domains)
    live = live.at[order[0]].set(blocks).at[order[1]].set(lowest)
    live_rows = live * EBLK
    chosen = jax.random.randint(fourth_key, (domains, EDGE_DEV), 0, ATOM_DEV)
    slots = jnp.arange(EDGE_DEV, dtype=jnp.int32)[None, :]
    masked = jnp.where(slots < live_rows[:, None], chosen, ATOM_DEV)
    return jnp.sort(masked, axis=1).reshape(-1)


def set_ends(values, own_key, smallest, top_value):
    spot = [jax.random.randint(jax.random.fold_in(own_key, axis), (), 0, length) for axis, length in enumerate(values.shape)]
    widest = values.shape.index(max(values.shape))
    beside = spot[:widest] + [(spot[widest] + 1) % values.shape[widest]] + spot[widest + 1:]
    return values.at[tuple(spot)].set(smallest).at[tuple(beside)].set(top_value)


def block_levels(stream_key, shape, shards, least, high):
    gain, own = 1.0, jax.random.fold_in(stream_key, 6)
    for dim, shards_of in shards:
        heights = jnp.exp(jax.random.uniform(jax.random.fold_in(own, dim), (shards_of,), jnp.float32, least / len(shards), high / len(shards)))
        gain = gain * jnp.repeat(heights, shape[dim] // shards_of).reshape([-1 if axis == dim else 1 for axis in range(len(shape))])
    return gain


def scatter_about(rng, extent, scale, bound, cuts=(), held_as=jnp.bfloat16):
    gain = block_levels(rng, extent, cuts, -0.22, 0.18) if cuts else 1.0
    values = jax.random.normal(rng, extent, jnp.float32) * scale * gain
    return jnp.minimum(jnp.maximum(values, -bound), bound).astype(held_as)


def setup_inputs(seed: int = 0) -> dict:
    key_list = jax.random.split(jax.random.key(seed), 17)
    features = scatter_about(key_list[0], (ATOMS, CH), 1.0, 6.0, ((0, 512),))
    positions = draw_positions(jax.random.fold_in(key_list[16], 71), 0)
    species = set_ends(jax.random.randint(key_list[2], (ATOMS,), 0, NSPEC), jax.random.fold_in(key_list[2], 1), 0, NSPEC - 1).astype(jnp.int32)
    ghost_list = set_ends(jax.random.randint(key_list[3], (N_ROW, N_SPACE * N_SPACE, CAP), 0, ATOM_DEV), jax.random.fold_in(key_list[3], 1), 0, ATOM_DEV - 1).astype(jnp.int32)
    edge_recv = draw_edge_recv(jax.random.fold_in(key_list[16], 71), 0)
    edge_send = set_ends(jax.random.randint(key_list[5], (EDGES,), 0, ATOM_DEV + N_SPACE * CAP), jax.random.fold_in(key_list[5], 1), 0, (ATOM_DEV + N_SPACE * CAP) - 1).astype(jnp.int32)
    edge_vec = draw_edge_vec(jax.random.fold_in(key_list[16], 71), 0)
    w_msg = scatter_about(key_list[7], (CH, 2 * CH), CH ** -0.5, 0.5)
    w_rad1 = scatter_about(key_list[8], (NRBF, CH), NRBF ** -0.5, 2.0, (), jnp.float32)
    w_rad2 = scatter_about(key_list[9], (CH, 2 * CH), CH ** -0.5, 0.5)
    w_up = scatter_about(key_list[10], (2 * CH, CH), (2 * CH) ** -0.5, 0.375)
    w_out = scatter_about(key_list[11], (CH,), CH ** -0.5, 0.5, (), jnp.float32)
    hardness = jnp.clip(jax.random.uniform(key_list[12], (NSPEC,), jnp.float32, 2.0, 4.0), 2.0, 4.0)
    width = jnp.clip(jax.random.uniform(key_list[13], (NSPEC,), jnp.float32, 0.8, 1.6), 0.8, 1.6)
    chi_shift = jnp.clip(jax.random.uniform(key_list[14], (NSPEC,), jnp.float32, -1.0, 1.0), -1.0, 1.0)
    field = jnp.clip(jnp.exp(jax.random.uniform(key_list[15], (1,), jnp.float32, math.log(0.01), math.log(0.03))), 0.01, 0.03)
    return {"features": features, "positions": positions, "species": species, "ghost_list": ghost_list, "edge_recv": edge_recv, "edge_send": edge_send, "edge_vec": edge_vec, "w_msg": w_msg, "w_rad1": w_rad1, "w_rad2": w_rad2, "w_up": w_up, "w_out": w_out, "hardness": hardness, "width": width, "chi_shift": chi_shift, "field": field}


cutoff = 6.0
message_scale = 0.125
two_over_root_pi = 2.0 / math.sqrt(math.pi)
inverse_root_pi = 1.0 / math.sqrt(math.pi)

def lookup(species, table):
    result = jnp.zeros(species.shape, jnp.float32)
    for kind in range(table.shape[0]):
        result = result + jnp.where(species == kind, table[kind], 0.0)
    return result

def pair_block(target, target_labels, source, source_labels, source_charge, forces):
    delta = target[:3, :, None] - source[:3, None, :]
    squared = lax.optimization_barrier(jnp.sum(delta * delta, axis=0))
    same = target_labels[:, None] == source_labels[None, :]
    squared = jnp.where(same, 1.0, squared)
    inverse = lax.rsqrt(squared)
    radius = squared * inverse
    spread = target[3][:, None] * target[3][:, None] + source[3][None, :] * source[3][None, :]
    scale = lax.rsqrt(2.0 * spread)
    scaled = radius * scale
    smear = lax.erf(scaled)
    if forces:
        slope = two_over_root_pi * scale * jnp.exp(-scaled * scaled) * inverse - smear * inverse * inverse
        weight = jnp.where(same, 0.0, source_charge[None, :] * slope * inverse)
        first = lax.optimization_barrier(jnp.sum(weight[None] * delta, axis=2))
        pairs = ((0, 0), (1, 1), (2, 2), (0, 1), (0, 2), (1, 2))
        second = jnp.stack([lax.optimization_barrier(jnp.sum(weight * delta[left] * delta[right], axis=1)) for left, right in pairs])
        return jnp.concatenate([first, second], axis=0)
    kernel = jnp.where(same, 0.0, smear * inverse)
    return lax.optimization_barrier(jnp.sum(kernel * source_charge[None, :], axis=1))

def edge_messages(sender_rows, vectors, projected, w_rad1, w_rad2):
    length = jnp.sqrt(lax.optimization_barrier(jnp.sum(vectors * vectors, axis=0)))
    unit = vectors / length
    order = jnp.arange(1, w_rad1.shape[0] + 1, dtype=jnp.int32).astype(jnp.float32)[:, None]
    ratio = length / cutoff
    envelope = (1.0 - ratio * ratio) * (1.0 - ratio * ratio)
    basis = jnp.sin(order * math.pi * ratio) / ratio * envelope
    radial = jax.nn.silu(jnp.dot(basis.T, w_rad1, precision=lax.Precision.HIGHEST)).astype(jnp.bfloat16)
    filters = jnp.dot(radial, w_rad2, preferred_element_type=jnp.float32)
    picked = jnp.take(projected, sender_rows, axis=0).astype(jnp.float32) * filters
    chans = w_rad1.shape[1]
    scalar = picked[:, :chans]
    carried = picked[:, chans:]
    joined = [scalar, unit[0][:, None] * carried, unit[1][:, None] * carried, unit[2][:, None] * carried]
    return jnp.concatenate(joined, axis=1).astype(jnp.bfloat16)

def reference(features, positions, species, ghost_list, edge_recv, edge_send, edge_vec, w_msg, w_rad1, w_rad2, w_up, w_out, hardness, width, chi_shift, field):
    domains = N_ROW * N_SPACE
    grouped = features.reshape(N_ROW, N_SPACE, ATOM_DEV, CH)
    lists = ghost_list.reshape(N_ROW, N_SPACE, N_SPACE, CAP)

    def pick_rows(rows, chosen):
        return jnp.take(rows, chosen.reshape(-1), axis=0).reshape(N_SPACE, CAP, CH)
    picked = jax.vmap(jax.vmap(pick_rows))(grouped, lists)
    ghosts = picked.transpose(0, 2, 1, 3, 4).reshape(domains, N_SPACE * CAP, CH)
    owned = features.reshape(domains, ATOM_DEV, CH)
    receive = edge_recv.reshape(domains, EDGE_DEV)
    senders = edge_send.reshape(domains, EDGE_DEV)
    vectors = edge_vec.reshape(3, domains, EDGE_DEV).transpose(1, 0, 2)

    def one_domain(item):
        own_rows, ghost_rows, targets, sources, displace = item
        table = jnp.concatenate([own_rows, ghost_rows], axis=0)
        projected = jnp.dot(table, w_msg, preferred_element_type=jnp.float32).astype(jnp.bfloat16)
        message = edge_messages(sources, displace, projected, w_rad1, w_rad2)
        totals = jax.ops.segment_sum(message.astype(jnp.float32), targets, num_segments=ATOM_DEV + 1)
        return totals[:ATOM_DEV]
    summed = lax.map(one_domain, (owned, ghosts, receive, senders, vectors)).reshape(ATOMS, 4 * CH)
    summed = summed * message_scale
    vector_part = summed[:, CH:].reshape(ATOMS, 3, CH)
    invariant = jnp.concatenate([summed[:, :CH], lax.optimization_barrier(jnp.sum(vector_part * vector_part, axis=1))], axis=1).astype(jnp.bfloat16)
    hidden = jax.nn.silu(jnp.dot(invariant, w_up, preferred_element_type=jnp.float32))
    new_features = (features.astype(jnp.float32) + hidden).astype(jnp.bfloat16)
    chi = jnp.dot(hidden, w_out, precision=lax.Precision.HIGHEST) + lookup(species, chi_shift)
    sigma = lookup(species, width)
    diag = lookup(species, hardness) + inverse_root_pi / sigma
    placed = jnp.concatenate([positions, sigma[None, :]], axis=0)
    labels = jnp.arange(ATOMS, dtype=jnp.int32)
    block = min(ATOMS, 256)
    target_blocks = placed.reshape(4, ATOMS // block, block).transpose(1, 0, 2)
    label_blocks = labels.reshape(ATOMS // block, block)

    def couple(vector, forces):

        def one_block(item):
            return pair_block(item[0], item[1], placed, labels, vector, forces)
        result = lax.map(one_block, (target_blocks, label_blocks))
        if forces:
            return result.transpose(1, 0, 2).reshape(9, ATOMS)
        return result.reshape(ATOMS)
    rhs = field[0] * positions[2] - chi
    charges = jnp.zeros_like(rhs)
    residual = rhs
    direction = rhs
    norm_now = jnp.sum(residual * residual)
    for step in range(ITERS):
        image = diag * direction + couple(direction, False)
        alpha = norm_now / jnp.sum(direction * image)
        charges = charges + alpha * direction
        residual = residual - alpha * image
        fresh = jnp.sum(residual * residual)
        direction = residual + fresh / norm_now * direction
        norm_now = fresh
    sums = couple(charges, True)
    pull = -charges[None, :] * sums[:3]
    forces = jnp.concatenate([pull[:2], pull[2:] + (charges * field[0])[None, :]], axis=0)
    virial = 0.5 * charges[None, :] * sums[3:]
    return (new_features, charges, forces, virial)
```

```python
import functools
import math

import jax
import jax.numpy as jnp
from jax import lax
from jax.experimental import pallas as pl
from jax.experimental.pallas import tpu as pltpu
from jax.sharding import PartitionSpec as P

MESH = pl.DeviceIdType.MESH
NZ = 16
NS = 32
A = 16
L = 128
E = 512

CUTOFF = 6.0
MESSAGE_SCALE = 0.125
TWO_OVER_ROOT_PI = 2.0 / math.sqrt(math.pi)
INVERSE_ROOT_PI = 1.0 / math.sqrt(math.pi)

ERF_P = 0.45
ERF_C = (
    0.25898973,
    0.20100906,
    0.46017168,
    -0.37580456,
    0.85716943,
    -0.49410514,
    0.09256981,
)

X_LIST, X_FEAT, X_POS_Z, X_POS_P, X_B_Z, X_B_P, X_Y_Z, X_Y_P, X_S_Z, X_S_P = range(10)
EXCHANGES = 10

f32 = jnp.float32
bf16 = jnp.bfloat16


def iota(shape, dim):
    return lax.broadcasted_iota(jnp.int32, shape, dim)


def kernel(
    feat, pos, species, ghosts, recv, sender, evec, w_msg, w_rad1, w_rad2, w_up, w_out,
    hardness, width, chi_shift, field,
    nf_out, q_out, f_out, v_out,
    lists, list_in, feat_in, own_in, packet, zpos, line, ppos, zvec, pair, vecs, zsum, psum,
    fil, base, slot, first, columns, coords, green, slopes, part, rows9, send_sem, recv_sem,
):
    z = lax.axis_index("row")
    s = lax.axis_index("space")
    barrier = pltpu.get_barrier_semaphore()

    @pl.loop(1, NZ)
    def _(k):
        pl.semaphore_signal(
            barrier, inc=1, device_id=(lax.rem(z + k, NZ), s), device_id_type=MESH
        )

    @pl.loop(1, NS)
    def _(k):
        pl.semaphore_signal(
            barrier, inc=1, device_id=(z, lax.rem(s + k, NS)), device_id_type=MESH
        )

    def send_z(which, src, dst, rows):
        @pl.loop(1, NZ)
        def _(k):
            pltpu.make_async_remote_copy(
                src_ref=src,
                dst_ref=dst.at[pl.ds(z * rows, rows)],
                send_sem=send_sem.at[which],
                recv_sem=recv_sem.at[which],
                device_id=(lax.rem(z + k, NZ), s),
                device_id_type=MESH,
            ).start()

    def send_p(which, source, dst, rows):
        at = pl.multiple_of(s * rows, rows)

        @pl.loop(1, NS)
        def _(k):
            peer = lax.rem(s + k, NS)
            pltpu.make_async_remote_copy(
                src_ref=source(peer),
                dst_ref=dst.at[pl.ds(at, rows)],
                send_sem=send_sem.at[which],
                recv_sem=recv_sem.at[which],
                device_id=(z, peer),
                device_id_type=MESH,
            ).start()

    def await_rows(sem, dst, rows):
        some = dst.at[pl.ds(0, rows)]
        pltpu.make_async_copy(some, some, sem).wait()

    lane = iota((1, L), 1)
    half = z // 8
    off = lax.rem(z, 8) * A
    mine = (lane >= off) & (lane < off + A)
    diagonal = iota((A, L), 1) == iota((A, L), 0) + off

    def to_row(column):
        return jnp.sum(jnp.where(diagonal, column, 0.0), axis=0, keepdims=True)

    own_in[...] = jnp.zeros_like(own_in)
    own_in[0:3, 0:A] = pos[...]
    own_in[3:4, 0:A] = species[...].astype(f32)
    own = pltpu.roll(own_in[...], off, axis=1)
    kind = own[3:4]

    def lookup(table):
        out = jnp.zeros((1, L), f32)
        for k in range(4):
            out = out + jnp.where(mine & (kind == k), table[k], 0.0)
        return out

    sigma = jnp.where(mine, lookup(width), 1.0)
    diag = jnp.where(mine, lookup(hardness) + INVERSE_ROOT_PI / sigma, 0.0)
    packet[0:3, :] = own[0:3]
    packet[3:4, :] = jnp.where(mine, 2.0 * sigma * sigma, 0.0)
    packet[4:8, :] = jnp.zeros((4, L), f32)
    lists[...] = jnp.zeros_like(lists)
    lists[:, 0:NS] = ghosts[0]
    list_in[NS:, :] = jnp.zeros((L - NS, L), jnp.int32)

    vectors = evec[...]
    squared = vectors[0:1] * vectors[0:1] + vectors[1:2] * vectors[1:2] + vectors[2:3] * vectors[2:3]
    length = jnp.sqrt(squared)
    unit = vectors / length
    ratio = length / CUTOFF
    envelope = (1.0 - ratio * ratio) * (1.0 - ratio * ratio)
    order = (iota((8, 1), 0) + 1).astype(f32)
    basis = jnp.sin(order * math.pi * ratio) / ratio * envelope
    mixed = lax.dot_general(
        basis, w_rad1[...], (((0,), (0,)), ((), ())),
        precision=lax.Precision.HIGHEST, preferred_element_type=f32,
    )
    radial = jax.nn.silu(mixed).astype(bf16)
    filters = jnp.dot(radial, w_rad2[...], preferred_element_type=f32)
    slots = sender[...]
    local = slots < A
    ghost = slots - A
    columns[0:3, :] = unit
    columns[3:4, :] = jnp.where(local, s * A + slots, (ghost // NS) * A).astype(f32)
    columns[4:5, :] = jnp.where(local, -1, ghost // NS).astype(f32)
    columns[5:6, :] = lax.rem(jnp.where(local, 0, ghost), NS).astype(f32)
    columns[6:8, :] = jnp.zeros((2, E), f32)
    turned = columns[...].T
    fil[:, 0:L] = filters[:, 0:L]
    for c in range(3):
        fil[:, (c + 1) * L : (c + 2) * L] = filters[:, L:] * turned[:, c : c + 1]
    lane_f = iota((E, L), 1).astype(f32)
    base[...] = lane_f - turned[:, 3:4]
    first[...] = jnp.where(lane_f == turned[:, 4:5], 1.0, 0.0).astype(bf16)
    slot[...] = jnp.where(lane_f == turned[:, 5:6], 1.0, 0.0)
    receivers = jnp.where(iota((A, E), 0) == recv[...], 1.0, 0.0).astype(bf16)

    pl.semaphore_wait(barrier, NZ + NS - 2)
    send_p(X_LIST, lambda peer: lists.at[pl.ds(peer, 1)], list_in, 1)
    send_p(X_FEAT, lambda peer: feat, feat_in, A)
    send_z(X_POS_Z, packet.at[pl.ds(0, 4)], zpos, 4)
    list_in[pl.ds(s, 1), :] = lists[pl.ds(s, 1), :]
    feat_in[pl.ds(pl.multiple_of(s * A, A), A), :] = feat[...]
    zpos[pl.ds(z * 4, 4), :] = packet[0:4, :]

    await_rows(recv_sem.at[X_LIST], list_in, NS - 1)
    found = jnp.dot(first[...], list_in[...].astype(f32).astype(bf16), preferred_element_type=f32)
    found = (found * slot[...]).astype(bf16)
    found = jnp.dot(found, jnp.ones((L, L), bf16), preferred_element_type=f32)
    await_rows(recv_sem.at[X_FEAT], feat_in, (NS - 1) * A)
    offset = base[...] - found
    picks = jnp.concatenate(
        [jnp.where(offset == float(-L * g), 1.0, 0.0).astype(bf16) for g in range(4)], axis=1
    )
    picked = jnp.dot(picks, feat_in[...], preferred_element_type=f32).astype(bf16)
    projected = jnp.dot(picked, w_msg[...], preferred_element_type=f32).astype(bf16).astype(f32)
    lower, upper = projected[:, 0:L], projected[:, L:]
    message = jnp.concatenate(
        [(lower * fil[:, 0:L]).astype(bf16)]
        + [(upper * fil[:, (c + 1) * L : (c + 2) * L]).astype(bf16) for c in range(3)],
        axis=1,
    )
    summed = jnp.dot(receivers, message, preferred_element_type=f32) * MESSAGE_SCALE
    norms = summed[:, L : 2 * L] * summed[:, L : 2 * L]
    for c in range(2, 4):
        norms = norms + summed[:, c * L : (c + 1) * L] * summed[:, c * L : (c + 1) * L]
    invariant = jnp.concatenate([summed[:, 0:L], norms], axis=1).astype(bf16)
    hidden = jax.nn.silu(jnp.dot(invariant, w_up[...], preferred_element_type=f32))
    nf_out[...] = (feat[...].astype(f32) + hidden).astype(bf16)
    chi = to_row(jnp.sum(hidden * w_out[...], axis=1, keepdims=True)) + lookup(chi_shift)
    rhs = jnp.where(mine, field[0] * own[2:3] - chi, 0.0)

    def halves(k):
        return (
            jnp.sum(zvec[k, 0:8, :], axis=0, keepdims=True),
            jnp.sum(zvec[k, 8:16, :], axis=0, keepdims=True),
        )

    def start_gather(k, which, row):
        pair[k, 2:3, :] = row
        zvec[k, pl.ds(z, 1), :] = row
        send_z(which, pair.at[k, pl.ds(2, 1)], zvec.at[k], 1)

    def turn_gather(k, which, into):
        await_rows(recv_sem.at[which], zvec.at[k], NZ - 1)
        low, high = halves(k)
        pair[k, 0:1, :] = low
        pair[k, 1:2, :] = high
        send_p(into, lambda peer: pair.at[k, pl.ds(0, 2)], vecs.at[k], 2)
        vecs[k, pl.ds(2 * s, 1), :] = low
        vecs[k, pl.ds(2 * s + 1, 1), :] = high

    start_gather(0, X_B_Z, rhs)

    await_rows(recv_sem.at[X_POS_Z], zpos, (NZ - 1) * 4)
    for h in range(2):
        tiles = zpos[h * 32 : h * 32 + 8, :]
        for t in range(1, 4):
            tiles = tiles + zpos[h * 32 + 8 * t : h * 32 + 8 * t + 8, :]
        line[h * 4 : h * 4 + 4, :] = tiles[0:4] + tiles[4:8]
    send_p(X_POS_P, lambda peer: line, ppos, 8)
    ppos[pl.ds(pl.multiple_of(s * 8, 8), 8), :] = line[...]
    for h in range(2):
        for c in range(4):
            spread = jnp.broadcast_to(line[h * 4 + c : h * 4 + c + 1, :], (L, L))
            coords[c, h * L : (h + 1) * L, :] = spread.T

    turn_gather(0, X_B_Z, X_B_P)
    await_rows(recv_sem.at[X_POS_P], ppos, (NS - 1) * 8)
    where = [ppos[pl.ds(c, 64, stride=4), :] for c in range(4)]
    own_row = 2 * s + half

    @pl.loop(0, A)
    def _(i):
        at = [coords[c, pl.ds(z * A + i, 1), :] for c in range(4)]
        dx, dy, dz = (at[c] - where[c] for c in range(3))
        r2 = jnp.maximum(dx * dx + dy * dy + dz * dz, 1.0)
        inverse = lax.rsqrt(r2)
        scale = lax.rsqrt(at[3] + where[3])
        x = r2 * inverse * scale
        bell = jnp.exp(-x * x)
        t = 1.0 / (1.0 + ERF_P * x)
        poly = ERF_C[6]
        for c in ERF_C[5::-1]:
            poly = poly * t + c
        kernel_ij = (1.0 - bell * (poly * t)) * inverse
        green[i] = kernel_ij
        slopes[i] = inverse * inverse * (TWO_OVER_ROOT_PI * scale * bell - kernel_ij)
        green[i, pl.ds(own_row, 1), :] = jnp.where(
            lane == off + i, diag, green[i, pl.ds(own_row, 1), :]
        )

    def apply(vector):
        @pl.loop(0, A)
        def _(i):
            terms = green[i] * vector
            part[pl.ds(i, 1), :] = jnp.sum(terms, axis=0, keepdims=True)

        return to_row(jnp.sum(part[...], axis=1, keepdims=True))

    def total(value):
        return jnp.sum(jnp.sum(value, axis=0, keepdims=True), axis=1, keepdims=True)

    await_rows(recv_sem.at[X_B_P], vecs.at[0], (NS - 1) * 2)
    image = apply(vecs[0])
    start_gather(1, X_Y_Z, image)
    norm = total(vecs[0] * vecs[0])
    turn_gather(1, X_Y_Z, X_Y_P)
    await_rows(recv_sem.at[X_Y_P], vecs.at[1], (NS - 1) * 2)
    alpha = norm / total(vecs[0] * vecs[1])
    residual = vecs[0] - alpha * vecs[1]
    fresh = total(residual * residual)
    beta = fresh / norm
    vecs[2] = residual + beta * vecs[0]
    vecs[3] = alpha * vecs[0]
    step_row = (rhs - alpha * image) + beta * rhs
    second_image = apply(vecs[2])
    row = step_row * second_image
    pair[2, 2:3, :] = row
    zsum[pl.ds(z, 1), :] = row
    send_z(X_S_Z, pair.at[2, pl.ds(2, 1)], zsum, 1)

    def moments(part_id):
        @pl.loop(0, A)
        def _(i):
            at = [coords[c, pl.ds(z * A + i, 1), :] for c in range(3)]
            dx, dy, dz = (at[c] - where[c] for c in range(3))
            for v in range(2):
                weight = slopes[i] * vecs[3 - v]
                mx, my, mz = weight * dx, weight * dy, weight * dz
                outs = (mx, my, mz, mx * dx, my * dy, mz * dz, mx * dy, mx * dz, my * dz)
                for c, terms in enumerate(outs):
                    rows9[v, c, pl.ds(i, 1), :] = jnp.sum(terms, axis=0, keepdims=True)

    await_rows(recv_sem.at[X_S_Z], zsum, NZ - 1)
    row = jnp.sum(zsum[...], axis=0, keepdims=True)
    pair[3, 2:3, :] = row
    psum[pl.ds(s, 1), :] = row
    send_p(X_S_P, lambda peer: pair.at[3, pl.ds(2, 1)], psum, 1)
    moments(0)
    sums = [
        [to_row(jnp.sum(rows9[v, c], axis=1, keepdims=True)) for c in range(9)] for v in range(2)
    ]
    await_rows(recv_sem.at[X_S_P], psum, NS - 1)
    second_alpha = fresh / total(psum[...])
    charge = alpha * rhs + second_alpha * step_row
    moment = [sums[0][c] + second_alpha * sums[1][c] for c in range(9)]
    result = [charge]
    for c in range(3):
        force = -charge * moment[c]
        result.append(force + charge * field[0] if c == 2 else force)
    for c in range(3, 9):
        result.append(0.5 * charge * moment[c])
    result = jnp.concatenate(result + [jnp.zeros((6, L), f32)], axis=0)
    result = pltpu.roll(result, lax.rem(L - off, L), axis=1)
    q_out[...] = result[0:1, 0:A]
    f_out[...] = result[1:4, 0:A]
    v_out[...] = result[4:10, 0:A]

    for which, dst, rows in (
        (X_LIST, list_in, NS - 1),
        (X_FEAT, feat_in, (NS - 1) * A),
        (X_POS_Z, zpos, (NZ - 1) * 4),
        (X_POS_P, ppos, (NS - 1) * 8),
        (X_B_Z, zvec.at[0], NZ - 1),
        (X_B_P, vecs.at[0], (NS - 1) * 2),
        (X_Y_Z, zvec.at[1], NZ - 1),
        (X_Y_P, vecs.at[1], (NS - 1) * 2),
        (X_S_Z, zsum, NZ - 1),
        (X_S_P, psum, NS - 1),
    ):
        await_rows(send_sem.at[which], dst, rows)


def shards(
    features, positions, species, ghost_list, edge_recv, edge_send, edge_vec,
    w_msg, w_rad1, w_rad2, w_up, w_out, hardness, width, chi_shift, field,
):
    vmem = pl.BlockSpec(memory_space=pltpu.VMEM)
    smem = pl.BlockSpec(memory_space=pltpu.SMEM)
    new_features, charges, forces, virial = pl.pallas_call(
        kernel,
        out_shape=(
            jax.ShapeDtypeStruct((A, L), bf16),
            jax.ShapeDtypeStruct((1, A), f32),
            jax.ShapeDtypeStruct((3, A), f32),
            jax.ShapeDtypeStruct((6, A), f32),
        ),
        in_specs=[vmem] * 12 + [smem] * 4,
        out_specs=[vmem] * 4,
        scratch_shapes=[
            pltpu.VMEM((NS, L), jnp.int32),
            pltpu.VMEM((L, L), jnp.int32),
            pltpu.VMEM((NS * A, L), bf16),
            pltpu.VMEM((8, L), f32),
            pltpu.VMEM((8, L), f32),
            pltpu.VMEM((NZ * 4, L), f32),
            pltpu.VMEM((8, L), f32),
            pltpu.VMEM((NS * 8, L), f32),
            pltpu.VMEM((2, NZ, L), f32),
            pltpu.VMEM((4, 8, L), f32),
            pltpu.VMEM((4, 2 * NS, L), f32),
            pltpu.VMEM((NZ, L), f32),
            pltpu.VMEM((NS, L), f32),
            pltpu.VMEM((E, 4 * L), f32),
            pltpu.VMEM((E, L), f32),
            pltpu.VMEM((E, L), f32),
            pltpu.VMEM((E, L), bf16),
            pltpu.VMEM((8, E), f32),
            pltpu.VMEM((4, 2 * L, L), f32),
            pltpu.VMEM((A, 2 * NS, L), f32),
            pltpu.VMEM((A, 2 * NS, L), f32),
            pltpu.VMEM((A, L), f32),
            pltpu.VMEM((2, 9, A, L), f32),
            pltpu.SemaphoreType.DMA((EXCHANGES,)),
            pltpu.SemaphoreType.DMA((EXCHANGES,)),
        ],
        compiler_params=pltpu.CompilerParams(
            collective_id=0, has_side_effects=True, vmem_limit_bytes=32 * 1024 * 1024
        ),
    )(
        features, positions, species.reshape(1, A), ghost_list,
        edge_recv.reshape(1, E), edge_send.reshape(1, E), edge_vec,
        w_msg, w_rad1, w_rad2, w_up, w_out.reshape(1, L), hardness, width, chi_shift, field,
    )
    return new_features, charges.reshape(A), forces, virial


def solution(mesh):
    atoms = P(("row", "space"))
    columns = P(None, ("row", "space"))
    return jax.shard_map(
        shards,
        mesh=mesh,
        in_specs=(
            P(("row", "space"), None), columns, atoms, P("row", "space", None), atoms, atoms, columns,
        )
        + (P(),) * 9,
        out_specs=(P(("row", "space"), None), atoms, columns, columns),
        check_vma=False,
    )
```

```python
import functools
import math

import jax
import jax.numpy as jnp
from jax import lax
from jax.experimental import pallas as pl
from jax.experimental.pallas import tpu as pltpu
from jax.sharding import PartitionSpec as P

MESH = pl.DeviceIdType.MESH
NZ = 16
NS = 32
A = 16
L = 128
E = 512

CUTOFF = 6.0
MESSAGE_SCALE = 0.125
TWO_OVER_ROOT_PI = 2.0 / math.sqrt(math.pi)
INVERSE_ROOT_PI = 1.0 / math.sqrt(math.pi)

ERF_P = 0.55
ERF_C = (0.30158329, 0.39084308, -0.04142873, 0.75971775, -0.51804038, 0.10732501)

X_LIST, X_FEAT, X_POS_Z, X_B_Z, X_B_P, X_Y, X_S, X_POS_P = range(8)
GROUPS = 8
EXCHANGES = X_POS_P + GROUPS
GROUP_ORDER = (0, 2, 6, 1, 4, 3, 7, 5)
EARLY = 4

f32 = jnp.float32
bf16 = jnp.bfloat16


def iota(shape, dim):
    return lax.broadcasted_iota(jnp.int32, shape, dim)


def reciprocal(x):
    guess = pl.reciprocal(x, approx=True)
    return guess * (2.0 - x * guess)


def smeared(r2, spread):
    inverse = lax.rsqrt(r2)
    scale = lax.rsqrt(spread)
    x = r2 * inverse * scale
    bell = jnp.exp(-(x * x))
    t = reciprocal(1.0 + ERF_P * x)
    poly = ERF_C[5]
    for c in ERF_C[4::-1]:
        poly = poly * t + c
    return (1.0 - bell * (poly * t)) * inverse, TWO_OVER_ROOT_PI * scale * bell, inverse


def kernel(*refs):
    given = refs[:16]
    nf_out, result_out = refs[16:18]
    held = refs[18:34]
    (
        lists, list_in, feat_in, own_in, packet, zpos, line, ppos, zvec, pair, vecs, psum,
        fil, base, slot, first, columns, coords, own_at, green, part, rows9,
        send_sem, recv_sem, in_sem,
    ) = refs[34:]
    (
        feat, pos, species, ghosts, recv, sender, evec, w_msg, w_rad1, w_rad2, w_up, w_out,
        hardness, width, chi_shift, field,
    ) = held
    z = lax.axis_index("row")
    s = lax.axis_index("space")
    twin = z + 1 - 2 * lax.rem(z, 2)
    barrier = pltpu.get_barrier_semaphore()

    def signal(device):
        pl.semaphore_signal(barrier, inc=1, device_id=device, device_id_type=MESH)

    @pl.loop(1, NZ)
    def _(k):
        signal((lax.rem(z + k, NZ), s))

    @pl.loop(1, NS)
    def _(k):
        signal((z, lax.rem(s + k, NS)))
        signal((twin, lax.rem(s + k, NS)))

    loads = [pltpu.make_async_copy(given[k], held[k], in_sem.at[k]) for k in range(16)]
    for load in loads:
        load.start()

    def send(which, source, destination, device):
        pltpu.make_async_remote_copy(
            src_ref=source,
            dst_ref=destination,
            send_sem=send_sem.at[which],
            recv_sem=recv_sem.at[which],
            device_id=device,
            device_id_type=MESH,
        ).start()

    def send_z(which, src, dst, rows):
        @pl.loop(1, NZ)
        def _(k):
            send(which, src, dst.at[pl.ds(z * rows, rows)], (lax.rem(z + k, NZ), s))

    def send_p(which, source, dst, rows):
        at = pl.multiple_of(s * rows, rows)

        @pl.loop(1, NS)
        def _(k):
            peer = lax.rem(s + k, NS)
            send(which, source(peer), dst.at[pl.ds(at, rows)], (z, peer))

    def send_two_planes(which, src, dst, at):
        send(which, src, dst.at[pl.ds(at, 1)], (twin, s))

        @pl.loop(1, NS)
        def _(k):
            peer = lax.rem(s + k, NS)
            send(which, src, dst.at[pl.ds(at, 1)], (twin, peer))
            send(which, src, dst.at[pl.ds(at, 1)], (z, peer))

    def await_rows(sem, dst, rows):
        some = dst.at[pl.ds(0, rows)]
        pltpu.make_async_copy(some, some, sem).wait()

    lane = iota((1, L), 1)
    half = z // 8
    off = lax.rem(z, 8) * A
    mine = (lane >= off) & (lane < off + A)
    diagonal = iota((A, L), 1) == iota((A, L), 0) + off
    chunk = lax.rem(z, 2)

    def to_row(column):
        return jnp.sum(jnp.where(diagonal, column, 0.0), axis=0, keepdims=True)

    for load in loads:
        load.wait()
    own_in[...] = jnp.zeros_like(own_in)
    own_in[0:3, 0:A] = pos[...]
    own_in[3:4, 0:A] = species[...].astype(f32)
    own = pltpu.roll(own_in[...], off, axis=1)
    kind = own[3:4]

    def lookup(table):
        out = jnp.zeros((1, L), f32)
        for k in range(4):
            out = out + jnp.where(mine & (kind == k), table[k], 0.0)
        return out

    sigma = jnp.where(mine, lookup(width), 1.0)
    spread = jnp.where(mine, 2.0 * sigma * sigma, 0.0)
    packet[0:3, :] = own[0:3]
    packet[3:4, :] = spread
    packet[4:5, :] = jnp.where(mine, lookup(hardness) + INVERSE_ROOT_PI / sigma, 0.0)
    packet[5:8, :] = jnp.zeros((3, L), f32)
    for c in range(4):
        column = jnp.sum(jnp.where(diagonal, packet[c : c + 1, :], 0.0), axis=1, keepdims=True)
        own_at[c] = jnp.broadcast_to(column, (A, L))
    lists[...] = jnp.zeros_like(lists)
    lists[:, 0:NS] = ghosts[0]
    list_in[NS:, :] = jnp.zeros((L - NS, L), jnp.int32)

    vectors = evec[...]
    squared = vectors[0:1] * vectors[0:1] + vectors[1:2] * vectors[1:2] + vectors[2:3] * vectors[2:3]
    length = jnp.sqrt(squared)
    unit = vectors / length
    ratio = length / CUTOFF
    envelope = (1.0 - ratio * ratio) * (1.0 - ratio * ratio)
    order = (iota((8, 1), 0) + 1).astype(f32)
    basis = jnp.sin(order * math.pi * ratio) / ratio * envelope
    mixed = lax.dot_general(
        basis, w_rad1[...], (((0,), (0,)), ((), ())),
        precision=lax.Precision.HIGHEST, preferred_element_type=f32,
    )
    radial = jax.nn.silu(mixed).astype(bf16)
    filters = jnp.dot(radial, w_rad2[...], preferred_element_type=f32)
    slots = sender[...]
    local = slots < A
    ghost = slots - A
    columns[0:3, :] = unit
    columns[3:4, :] = jnp.where(local, s * A + slots, (ghost // NS) * A).astype(f32)
    columns[4:5, :] = jnp.where(local, -1, ghost // NS).astype(f32)
    columns[5:6, :] = lax.rem(jnp.where(local, 0, ghost), NS).astype(f32)
    columns[6:8, :] = jnp.zeros((2, E), f32)
    turned = columns[...].T
    fil[:, 0:L] = filters[:, 0:L]
    for c in range(3):
        fil[:, (c + 1) * L : (c + 2) * L] = filters[:, L:] * turned[:, c : c + 1]
    lane_f = iota((E, L), 1).astype(f32)
    base[...] = lane_f - turned[:, 3:4]
    first[...] = jnp.where(lane_f == turned[:, 4:5], 1.0, 0.0).astype(bf16)
    slot[...] = jnp.where(lane_f == turned[:, 5:6], 1.0, 0.0)
    receivers = jnp.where(iota((A, E), 0) == recv[...], 1.0, 0.0).astype(bf16)

    pl.semaphore_wait(barrier, NZ + 2 * NS - 3)
    send_p(X_LIST, lambda peer: lists.at[pl.ds(peer, 1)], list_in, 1)
    send_p(X_FEAT, lambda peer: feat, feat_in, A)
    send_z(X_POS_Z, packet, zpos, 8)
    list_in[pl.ds(s, 1), :] = lists[pl.ds(s, 1), :]
    feat_in[pl.ds(pl.multiple_of(s * A, A), A), :] = feat[...]
    zpos[pl.ds(pl.multiple_of(z * 8, 8), 8), :] = packet[...]

    await_rows(recv_sem.at[X_LIST], list_in, NS - 1)
    found = jnp.dot(first[...], list_in[...].astype(f32).astype(bf16), preferred_element_type=f32)
    found = (found * slot[...]).astype(bf16)
    found = jnp.dot(found, jnp.ones((L, L), bf16), preferred_element_type=f32)
    await_rows(recv_sem.at[X_FEAT], feat_in, (NS - 1) * A)
    offset = base[...] - found
    picks = jnp.concatenate(
        [jnp.where(offset == float(-L * g), 1.0, 0.0).astype(bf16) for g in range(4)], axis=1
    )
    picked = jnp.dot(picks, feat_in[...], preferred_element_type=f32).astype(bf16)
    projected = jnp.dot(picked, w_msg[...], preferred_element_type=f32).astype(bf16).astype(f32)
    lower, upper = projected[:, 0:L], projected[:, L:]
    message = jnp.concatenate(
        [(lower * fil[:, 0:L]).astype(bf16)]
        + [(upper * fil[:, (c + 1) * L : (c + 2) * L]).astype(bf16) for c in range(3)],
        axis=1,
    )
    summed = jnp.dot(receivers, message, preferred_element_type=f32) * MESSAGE_SCALE
    norms = summed[:, L : 2 * L] * summed[:, L : 2 * L]
    for c in range(2, 4):
        norms = norms + summed[:, c * L : (c + 1) * L] * summed[:, c * L : (c + 1) * L]
    invariant = jnp.concatenate([summed[:, 0:L], norms], axis=1).astype(bf16)
    hidden = jax.nn.silu(jnp.dot(invariant, w_up[...], preferred_element_type=f32))
    nf_out[...] = (feat[...].astype(f32) + hidden).astype(bf16)
    chi = to_row(jnp.sum(hidden * w_out[...], axis=1, keepdims=True)) + lookup(chi_shift)
    rhs = jnp.where(mine, field[0] * own[2:3] - chi, 0.0)

    pair[2:3, :] = rhs
    zvec[pl.ds(z, 1), :] = rhs
    send_z(X_B_Z, pair.at[pl.ds(2, 1)], zvec, 1)

    await_rows(recv_sem.at[X_POS_Z], zpos, (NZ - 1) * 8)
    for h in range(2):
        tile = zpos[h * 64 : h * 64 + 8, :]
        for t in range(1, 8):
            tile = tile + zpos[h * 64 + 8 * t : h * 64 + 8 * t + 8, :]
        line[h * 4 : h * 4 + 4, :] = tile[0:4]
        line[8 + h : 9 + h, :] = tile[4:5]
    own_group = s // 4

    @pl.loop(1, NS)
    def _(k):
        peer = lax.rem(s + k, NS)
        send(
            X_POS_P + own_group, line.at[pl.ds(0, 8)],
            ppos.at[pl.ds(pl.multiple_of(s * 8, 8), 8)], (z, peer),
        )

    ppos[pl.ds(pl.multiple_of(s * 8, 8), 8), :] = line[0:8, :]
    for c in range(4):
        spread_out = jnp.broadcast_to(line[pl.ds(chunk * 4 + c, 1), :], (L, L))
        coords[c] = spread_out.T
    diag_row = line[pl.ds(8 + chunk, 1), :]
    own_at_row = lax.rem(2 * s + chunk, 8)

    def fill(turn):
        group = own_group ^ GROUP_ORDER[turn]
        await_rows(recv_sem.at[X_POS_P + group], ppos, (3 if turn == 0 else 4) * 8)
        xs = [ppos[pl.ds(group * 32 + c, 8, stride=4), :] for c in range(4)]
        at_row = pl.multiple_of(group * 8, 8)

        @pl.loop(0, L, step=8)
        def _(i0):
            for i in range(8):
                at = [coords[c, pl.ds(i0 + i, 1), :] for c in range(4)]
                dx, dy, dz = (at[c] - xs[c] for c in range(3))
                r2 = jnp.maximum(dx * dx + dy * dy + dz * dz, 1.0)
                value = smeared(r2, at[3] + xs[3])[0]
                if turn == 0:
                    itself = (iota((8, L), 0) == own_at_row) & (iota((8, L), 1) == i0 + i)
                    value = jnp.where(itself, diag_row, value)
                green[i0 + i, pl.ds(at_row, 8), :] = value

    for turn in range(EARLY):
        fill(turn)
    await_rows(recv_sem.at[X_B_Z], zvec, NZ - 1)
    low = jnp.sum(zvec[0:8, :], axis=0, keepdims=True)
    high = jnp.sum(zvec[8:16, :], axis=0, keepdims=True)
    pair[0:1, :] = low
    pair[1:2, :] = high
    send_p(X_B_P, lambda peer: pair.at[pl.ds(0, 2)], vecs.at[0], 2)
    vecs[0, pl.ds(2 * s, 1), :] = low
    vecs[0, pl.ds(2 * s + 1, 1), :] = high
    for turn in range(EARLY, GROUPS):
        fill(turn)

    chunk_row = 2 * s + chunk

    def apply(vector):
        @pl.loop(0, L, step=4)
        def _(i0):
            for i in range(4):
                terms = green[i0 + i] * vector
                part[pl.ds(i0 + i, 1), :] = jnp.sum(terms, axis=0, keepdims=True)

        return jnp.sum(part[...].T, axis=0, keepdims=True)

    def total(value):
        return jnp.sum(jnp.sum(value, axis=0, keepdims=True), axis=1, keepdims=True)

    await_rows(recv_sem.at[X_B_P], vecs.at[0], (NS - 1) * 2)
    rhs_all = vecs[0]
    image = apply(rhs_all)
    pair[3:4, :] = image
    vecs[1, pl.ds(chunk_row, 1), :] = image
    send_two_planes(X_Y, pair.at[pl.ds(3, 1)], vecs.at[1], chunk_row)
    norm = total(rhs_all * rhs_all)
    await_rows(recv_sem.at[X_Y], vecs.at[1], 2 * NS - 1)
    image_all = vecs[1]
    alpha = norm / total(rhs_all * image_all)
    residual = rhs_all - alpha * image_all
    fresh = total(residual * residual)
    beta = fresh / norm
    vecs[2] = residual + beta * rhs_all
    vecs[3] = alpha * rhs_all
    row = vecs[2, pl.ds(chunk_row, 1), :] * apply(vecs[2])
    pair[4:5, :] = row
    psum[pl.ds(chunk_row, 1), :] = row
    send_two_planes(X_S, pair.at[pl.ds(4, 1)], psum, chunk_row)

    where = [ppos[pl.ds(c, 64, stride=4), :] for c in range(4)]

    @pl.loop(0, A)
    def _(i):
        at = [own_at[c, pl.ds(i, 1), :] for c in range(4)]
        dx, dy, dz = (at[c] - where[c] for c in range(3))
        r2 = jnp.maximum(dx * dx + dy * dy + dz * dz, 1.0)
        value, peak, inverse = smeared(r2, at[3] + where[3])
        slope = inverse * inverse * (peak - value)
        for v in range(2):
            weight = slope * vecs[3 - v]
            mx, my, mz = weight * dx, weight * dy, weight * dz
            outs = (mx, my, mz, mx * dx, my * dy, mz * dz, mx * dy, mx * dz, my * dz)
            for c, terms in enumerate(outs):
                rows9[v, c, pl.ds(i, 1), :] = jnp.sum(terms, axis=0, keepdims=True)

    sums = [
        [to_row(jnp.sum(rows9[v, c], axis=1, keepdims=True)) for c in range(9)] for v in range(2)
    ]
    own_row = 2 * s + half
    await_rows(recv_sem.at[X_S], psum, 2 * NS - 1)
    second_alpha = fresh / total(psum[...])
    charge = vecs[3, pl.ds(own_row, 1), :] + second_alpha * vecs[2, pl.ds(own_row, 1), :]
    moment = [sums[0][c] + second_alpha * sums[1][c] for c in range(9)]
    result = []
    for c in range(3):
        force = -charge * moment[c]
        result.append(force + charge * field[0] if c == 2 else force)
    result.append(charge)
    result.append(jnp.zeros((4, L), f32))
    for c in range(3, 9):
        result.append(0.5 * charge * moment[c])
    result.append(jnp.zeros((2, L), f32))
    result = jnp.concatenate(result, axis=0)
    result_out[...] = pltpu.roll(result, lax.rem(L - off, L), axis=1)

    for which, dst, rows in (
        (X_LIST, list_in, NS - 1),
        (X_FEAT, feat_in, (NS - 1) * A),
        (X_POS_Z, zpos, (NZ - 1) * 8),
        (X_POS_P + own_group, ppos, (NS - 1) * 8),
        (X_B_Z, zvec, NZ - 1),
        (X_B_P, vecs.at[0], (NS - 1) * 2),
        (X_Y, vecs.at[1], 2 * NS - 1),
        (X_S, psum, 2 * NS - 1),
    ):
        await_rows(send_sem.at[which], dst, rows)


def hand_out(nf, result, nf_out, q_out, f_out, v_out, q, f, v, sem):
    q[...] = result[3:4, 0:A]
    f[...] = result[0:3, 0:A]
    v[...] = result[8:14, 0:A]
    copies = [
        pltpu.make_async_copy(a, b, sem.at[k])
        for k, (a, b) in enumerate(((nf, nf_out), (q, q_out), (f, f_out), (v, v_out)))
    ]
    for copy in copies:
        copy.start()
    for copy in copies:
        copy.wait()


def shards(*given):
    given = list(given)
    for k, shape in ((2, (1, A)), (4, (1, E)), (5, (1, E)), (11, (1, L))):
        given[k] = given[k].reshape(shape)
    vmem = pl.BlockSpec(memory_space=pltpu.VMEM)
    hbm = pl.BlockSpec(memory_space=pltpu.HBM)
    held = [pltpu.VMEM(x.shape, x.dtype) for x in given[:12]]
    held += [pltpu.SMEM(x.shape, x.dtype) for x in given[12:]]
    new_features, result = pl.pallas_call(
        kernel,
        out_shape=(jax.ShapeDtypeStruct((A, L), bf16), jax.ShapeDtypeStruct((16, L), f32)),
        in_specs=[hbm] * 16,
        out_specs=[vmem] * 2,
        scratch_shapes=held
        + [
            pltpu.VMEM((NS, L), jnp.int32),
            pltpu.VMEM((L, L), jnp.int32),
            pltpu.VMEM((NS * A, L), bf16),
            pltpu.VMEM((8, L), f32),
            pltpu.VMEM((8, L), f32),
            pltpu.VMEM((NZ * 8, L), f32),
            pltpu.VMEM((16, L), f32),
            pltpu.VMEM((NS * 8, L), f32),
            pltpu.VMEM((NZ, L), f32),
            pltpu.VMEM((8, L), f32),
            pltpu.VMEM((4, 2 * NS, L), f32),
            pltpu.VMEM((2 * NS, L), f32),
            pltpu.VMEM((E, 4 * L), f32),
            pltpu.VMEM((E, L), f32),
            pltpu.VMEM((E, L), f32),
            pltpu.VMEM((E, L), bf16),
            pltpu.VMEM((8, E), f32),
            pltpu.VMEM((4, L, L), f32),
            pltpu.VMEM((4, A, L), f32),
            pltpu.VMEM((L, 2 * NS, L), f32),
            pltpu.VMEM((L, L), f32),
            pltpu.VMEM((2, 9, A, L), f32),
            pltpu.SemaphoreType.DMA((EXCHANGES,)),
            pltpu.SemaphoreType.DMA((EXCHANGES,)),
            pltpu.SemaphoreType.DMA((16,)),
        ],
        compiler_params=pltpu.CompilerParams(
            collective_id=0, has_side_effects=True, vmem_limit_bytes=60 * 1024 * 1024
        ),
    )(*given)
    new_features, charges, forces, virial = pl.pallas_call(
        hand_out,
        out_shape=(
            jax.ShapeDtypeStruct((A, L), bf16),
            jax.ShapeDtypeStruct((1, A), f32),
            jax.ShapeDtypeStruct((3, A), f32),
            jax.ShapeDtypeStruct((6, A), f32),
        ),
        in_specs=[vmem] * 2,
        out_specs=[hbm] * 4,
        scratch_shapes=[
            pltpu.VMEM((1, A), f32),
            pltpu.VMEM((3, A), f32),
            pltpu.VMEM((6, A), f32),
            pltpu.SemaphoreType.DMA((4,)),
        ],
    )(new_features, result)
    return new_features, charges.reshape(A), forces, virial


def solution(mesh):
    atoms = P(("row", "space"))
    columns = P(None, ("row", "space"))
    return jax.shard_map(
        shards,
        mesh=mesh,
        in_specs=(
            P(("row", "space"), None), columns, atoms, P("row", "space", None), atoms, atoms, columns,
        )
        + (P(),) * 9,
        out_specs=(P(("row", "space"), None), atoms, columns, columns),
        check_vma=False,
    )
```

```python
import functools
import math

import jax
import jax.numpy as jnp
from jax import lax
from jax.experimental import pallas as pl
from jax.experimental.pallas import tpu as pltpu
from jax.sharding import PartitionSpec as P

MESH = pl.DeviceIdType.MESH
NZ = 16
NS = 32
A = 16
L = 128
E = 512

CUTOFF = 6.0
MESSAGE_SCALE = 0.125
TWO_OVER_ROOT_PI = 2.0 / math.sqrt(math.pi)
INVERSE_ROOT_PI = 1.0 / math.sqrt(math.pi)

ERF_P = 0.55
ERF_C = (0.30158329, 0.39084308, -0.04142873, 0.75971775, -0.51804038, 0.10732501)

X_LIST, X_FEAT, X_POS_Z, X_B_Z, X_B_P, X_Y, X_S, X_POS_P = range(8)
GROUPS = 8
EXCHANGES = X_POS_P + GROUPS
GROUP_ORDER = (0, 2, 6, 1, 4, 3, 7, 5)
EARLY = 2


def hops(k):
    return (0, 1, 2, 1)[k // 8] + (0, 1, 2, 1)[k // 2 % 4] + 0.3 * (k % 2)


PEERS = sorted(range(1, NS), key=hops, reverse=True)
PAIR_PEERS = sorted(
    [(other, k) for other in (0, 1) for k in range(NS) if other or k],
    key=lambda at: at[0] + hops(at[1]),
    reverse=True,
)

f32 = jnp.float32
bf16 = jnp.bfloat16


def iota(shape, dim):
    return lax.broadcasted_iota(jnp.int32, shape, dim)


def reciprocal(x):
    guess = pl.reciprocal(x, approx=True)
    return guess * (2.0 - x * guess)


def smeared(r2, spread):
    inverse = lax.rsqrt(r2)
    scale = lax.rsqrt(spread)
    x = r2 * inverse * scale
    bell = jnp.exp(-(x * x))
    t = reciprocal(1.0 + ERF_P * x)
    poly = ERF_C[5]
    for c in ERF_C[4::-1]:
        poly = poly * t + c
    return (1.0 - bell * (poly * t)) * inverse, TWO_OVER_ROOT_PI * scale * bell, inverse


def kernel(*refs):
    given = refs[:16]
    nf_out, q_out, f_out, v_out = refs[16:20]
    held = refs[20:36]
    (
        lists, list_in, feat_in, own_in, packet, zpos, line, ppos, zvec, pair, vecs, psum,
        fil, base, slot, first, columns, coords, own_at, green, part, rows9,
        send_sem, recv_sem, in_sem, plane_ready, line_ready,
    ) = refs[36:]
    (
        feat, pos, species, ghosts, recv, sender, evec, w_msg, w_rad1, w_rad2, w_up, w_out,
        hardness, width, chi_shift, field,
    ) = held
    z = lax.axis_index("row")
    s = lax.axis_index("space")
    twin = z + 1 - 2 * lax.rem(z, 2)
    barrier = pltpu.get_barrier_semaphore()

    def signal(device):
        pl.semaphore_signal(barrier, inc=1, device_id=device, device_id_type=MESH)

    even = lax.rem(s, 2) == 0
    mate = s + 1 - 2 * lax.rem(s, 2)

    @pl.loop(0, NS // 2)
    def _(k):
        peer = 2 * lax.rem(s // 2 + k, NS // 2)

        @pl.when(peer != s)
        def _():
            signal((z, peer))

    @pl.loop(1, NZ)
    def _(k):
        signal((lax.rem(z + k, NZ), (s // 2) * 2 + 1))

    @pl.when(even)
    def _():
        signal((z, mate))

    def tell(semaphore):
        pl.semaphore_signal(semaphore, inc=1, device_id=(z, mate), device_id_type=MESH)

    loads = [pltpu.make_async_copy(given[k], held[k], in_sem.at[k]) for k in range(16)]
    for load in loads:
        load.start()

    def send(which, source, destination, device):
        pltpu.make_async_remote_copy(
            src_ref=source,
            dst_ref=destination,
            send_sem=send_sem.at[which],
            recv_sem=recv_sem.at[which],
            device_id=device,
            device_id_type=MESH,
        ).start()

    def send_z(which, src, dst, rows):
        to = dst.at[pl.ds(z * rows, rows)]
        send(which, src, to, (lax.rem(z + 8, NZ), s))

        @pl.loop(1, 8)
        def _(k):
            send(which, src, to, (lax.rem(z + 8 - k, NZ), s))
            send(which, src, to, (lax.rem(z + 8 + k, NZ), s))

    def send_p(which, source, dst, rows):
        at = pl.multiple_of(s * rows, rows)
        for k in PEERS:
            send(which, source(s ^ k), dst.at[pl.ds(at, rows)], (z, s ^ k))

    def send_two_planes(which, src, dst, at):
        for other, k in PAIR_PEERS:
            send(which, src, dst.at[pl.ds(at, 1)], (twin if other else z, s ^ k))

    def await_rows(sem, dst, rows):
        some = dst.at[pl.ds(0, rows)]
        pltpu.make_async_copy(some, some, sem).wait()

    lane = iota((1, L), 1)
    half = z // 8
    off = lax.rem(z, 8) * A
    mine = (lane >= off) & (lane < off + A)
    diagonal = iota((A, L), 1) == iota((A, L), 0) + off
    chunk = lax.rem(z, 2)

    def to_row(column):
        return jnp.sum(jnp.where(diagonal, column, 0.0), axis=0, keepdims=True)

    for load in loads:
        load.wait()
    own_in[...] = jnp.zeros_like(own_in)
    own_in[0:3, 0:A] = pos[...]
    own_in[3:4, 0:A] = species[...].astype(f32)
    own = pltpu.roll(own_in[...], off, axis=1)
    kind = own[3:4]

    def lookup(table):
        out = jnp.zeros((1, L), f32)
        for k in range(4):
            out = out + jnp.where(mine & (kind == k), table[k], 0.0)
        return out

    sigma = jnp.where(mine, lookup(width), 1.0)
    spread = jnp.where(mine, 2.0 * sigma * sigma, 0.0)
    packet[0:3, :] = own[0:3]
    packet[3:4, :] = spread
    packet[4:5, :] = jnp.where(mine, lookup(hardness) + INVERSE_ROOT_PI / sigma, 0.0)
    packet[5:8, :] = jnp.zeros((3, L), f32)
    for c in range(4):
        column = jnp.sum(jnp.where(diagonal, packet[c : c + 1, :], 0.0), axis=1, keepdims=True)
        own_at[c] = jnp.broadcast_to(column, (A, L))
    lists[...] = jnp.zeros_like(lists)
    lists[:, 0:NS] = ghosts[0]
    list_in[NS:, :] = jnp.zeros((L - NS, L), jnp.int32)

    vectors = evec[...]
    squared = vectors[0:1] * vectors[0:1] + vectors[1:2] * vectors[1:2] + vectors[2:3] * vectors[2:3]
    length = jnp.sqrt(squared)
    unit = vectors / length
    ratio = length / CUTOFF
    envelope = (1.0 - ratio * ratio) * (1.0 - ratio * ratio)
    order = (iota((8, 1), 0) + 1).astype(f32)
    basis = jnp.sin(order * math.pi * ratio) / ratio * envelope
    mixed = lax.dot_general(
        basis, w_rad1[...], (((0,), (0,)), ((), ())),
        precision=lax.Precision.HIGHEST, preferred_element_type=f32,
    )
    radial = jax.nn.silu(mixed).astype(bf16)
    filters = jnp.dot(radial, w_rad2[...], preferred_element_type=f32)
    slots = sender[...]
    local = slots < A
    ghost = slots - A
    columns[0:3, :] = unit
    columns[3:4, :] = jnp.where(local, s * A + slots, (ghost // NS) * A).astype(f32)
    columns[4:5, :] = jnp.where(local, -1, ghost // NS).astype(f32)
    columns[5:6, :] = lax.rem(jnp.where(local, 0, ghost), NS).astype(f32)
    columns[6:8, :] = jnp.zeros((2, E), f32)

    @pl.when(even)
    def _():
        pl.semaphore_wait(barrier, NS - 1)
        tell(plane_ready)

    @pl.when(jnp.logical_not(even))
    def _():
        pl.semaphore_wait(plane_ready, 1)

    feat_at = pl.multiple_of(s * A, A)
    for k in PEERS:
        peer = s ^ k
        send(X_LIST, lists.at[pl.ds(peer, 1)], list_in.at[pl.ds(s, 1)], (z, peer))
        send(X_FEAT, feat, feat_in.at[pl.ds(feat_at, A)], (z, peer))
    turned = columns[...].T
    fil[:, 0:L] = filters[:, 0:L]
    for c in range(3):
        fil[:, (c + 1) * L : (c + 2) * L] = filters[:, L:] * turned[:, c : c + 1]
    lane_f = iota((E, L), 1).astype(f32)
    base[...] = lane_f - turned[:, 3:4]
    first[...] = jnp.where(lane_f == turned[:, 4:5], 1.0, 0.0).astype(bf16)
    slot[...] = jnp.where(lane_f == turned[:, 5:6], 1.0, 0.0)
    receivers = jnp.where(iota((A, E), 0) == recv[...], 1.0, 0.0).astype(bf16)

    @pl.when(even)
    def _():
        pl.semaphore_wait(line_ready, 1)

    @pl.when(jnp.logical_not(even))
    def _():
        pl.semaphore_wait(barrier, 2 * NZ - 1)
        tell(line_ready)

    send_z(X_POS_Z, packet, zpos, 8)
    list_in[pl.ds(s, 1), :] = lists[pl.ds(s, 1), :]
    feat_in[pl.ds(feat_at, A), :] = feat[...]
    zpos[pl.ds(pl.multiple_of(z * 8, 8), 8), :] = packet[...]

    await_rows(recv_sem.at[X_LIST], list_in, NS - 1)
    found = jnp.dot(first[...], list_in[...].astype(f32).astype(bf16), preferred_element_type=f32)
    found = (found * slot[...]).astype(bf16)
    found = jnp.dot(found, jnp.ones((L, L), bf16), preferred_element_type=f32)
    offset = base[...] - found
    picks = jnp.concatenate(
        [jnp.where(offset == float(-L * g), 1.0, 0.0).astype(bf16) for g in range(4)], axis=1
    )
    await_rows(recv_sem.at[X_FEAT], feat_in, (NS - 1) * A)
    table = jnp.dot(feat_in[...], w_msg[...], preferred_element_type=f32).astype(bf16)
    projected = jnp.dot(picks, table, preferred_element_type=f32)
    lower, upper = projected[:, 0:L], projected[:, L:]
    message = jnp.concatenate(
        [(lower * fil[:, 0:L]).astype(bf16)]
        + [(upper * fil[:, (c + 1) * L : (c + 2) * L]).astype(bf16) for c in range(3)],
        axis=1,
    )
    summed = jnp.dot(receivers, message, preferred_element_type=f32) * MESSAGE_SCALE
    norms = summed[:, L : 2 * L] * summed[:, L : 2 * L]
    for c in range(2, 4):
        norms = norms + summed[:, c * L : (c + 1) * L] * summed[:, c * L : (c + 1) * L]
    invariant = jnp.concatenate([summed[:, 0:L], norms], axis=1).astype(bf16)
    hidden = jax.nn.silu(jnp.dot(invariant, w_up[...], preferred_element_type=f32))
    nf_out[...] = (feat[...].astype(f32) + hidden).astype(bf16)
    chi = to_row(jnp.sum(hidden * w_out[...], axis=1, keepdims=True)) + lookup(chi_shift)
    rhs = jnp.where(mine, field[0] * own[2:3] - chi, 0.0)

    pair[2:3, :] = rhs
    zvec[pl.ds(z, 1), :] = rhs
    send_z(X_B_Z, pair.at[pl.ds(2, 1)], zvec, 1)

    await_rows(recv_sem.at[X_POS_Z], zpos, (NZ - 1) * 8)
    for h in range(2):
        tile = zpos[h * 64 : h * 64 + 8, :]
        for t in range(1, 8):
            tile = tile + zpos[h * 64 + 8 * t : h * 64 + 8 * t + 8, :]
        line[h * 4 : h * 4 + 4, :] = tile[0:4]
        line[8 + h : 9 + h, :] = tile[4:5]
    own_group = s // 4

    send_p(X_POS_P + own_group, lambda peer: line.at[pl.ds(0, 8)], ppos, 8)
    ppos[pl.ds(pl.multiple_of(s * 8, 8), 8), :] = line[0:8, :]
    for c in range(4):
        spread_out = jnp.broadcast_to(line[pl.ds(chunk * 4 + c, 1), :], (L, L))
        coords[c] = spread_out.T
    diag_row = line[pl.ds(8 + chunk, 1), :]
    own_at_row = lax.rem(2 * s + chunk, 8)

    def fill(turn):
        group = own_group ^ GROUP_ORDER[turn]
        await_rows(recv_sem.at[X_POS_P + group], ppos, (3 if turn == 0 else 4) * 8)
        xs = [ppos[pl.ds(group * 32 + c, 8, stride=4), :] for c in range(4)]
        at_row = pl.multiple_of(group * 8, 8)

        @pl.loop(0, L, step=8)
        def _(i0):
            for i in range(8):
                at = [coords[c, pl.ds(i0 + i, 1), :] for c in range(4)]
                dx, dy, dz = (at[c] - xs[c] for c in range(3))
                r2 = jnp.maximum(dx * dx + dy * dy + dz * dz, 1.0)
                value = smeared(r2, at[3] + xs[3])[0]
                if turn == 0:
                    itself = (iota((8, L), 0) == own_at_row) & (iota((8, L), 1) == i0 + i)
                    value = jnp.where(itself, diag_row, value)
                green[i0 + i, pl.ds(at_row, 8), :] = value

    for turn in range(EARLY):
        fill(turn)
    await_rows(recv_sem.at[X_B_Z], zvec, NZ - 1)
    low = jnp.sum(zvec[0:8, :], axis=0, keepdims=True)
    high = jnp.sum(zvec[8:16, :], axis=0, keepdims=True)
    pair[0:1, :] = low
    pair[1:2, :] = high
    send_p(X_B_P, lambda peer: pair.at[pl.ds(0, 2)], vecs.at[0], 2)
    vecs[0, pl.ds(2 * s, 1), :] = low
    vecs[0, pl.ds(2 * s + 1, 1), :] = high
    for turn in range(EARLY, GROUPS):
        fill(turn)

    chunk_row = 2 * s + chunk

    def apply(vector):
        @pl.loop(0, L, step=4)
        def _(i0):
            for i in range(4):
                terms = [
                    green[i0 + i, 8 * g : 8 * g + 8, :] * vector[8 * g : 8 * g + 8]
                    for g in range(GROUPS)
                ]
                while len(terms) > 1:
                    terms = [a + b for a, b in zip(terms[::2], terms[1::2])]
                part[pl.ds(pl.multiple_of((i0 + i) * 8, 8), 8), :] = terms[0]

        rows = [part[pl.ds(k, L, stride=8), :] for k in range(8)]
        while len(rows) > 1:
            rows = [a + b for a, b in zip(rows[::2], rows[1::2])]
        return jnp.sum(rows[0].T, axis=0, keepdims=True)

    def total(value):
        return jnp.sum(jnp.sum(value, axis=0, keepdims=True), axis=1, keepdims=True)

    await_rows(recv_sem.at[X_B_P], vecs.at[0], (NS - 1) * 2)
    rhs_all = vecs[0]
    image = apply(rhs_all)
    pair[3:4, :] = image
    vecs[1, pl.ds(chunk_row, 1), :] = image
    send_two_planes(X_Y, pair.at[pl.ds(3, 1)], vecs.at[1], chunk_row)
    norm = total(rhs_all * rhs_all)
    await_rows(recv_sem.at[X_Y], vecs.at[1], 2 * NS - 1)
    image_all = vecs[1]
    alpha = norm / total(rhs_all * image_all)
    residual = rhs_all - alpha * image_all
    fresh = total(residual * residual)
    beta = fresh / norm
    vecs[2] = residual + beta * rhs_all
    vecs[3] = alpha * rhs_all
    row = vecs[2, pl.ds(chunk_row, 1), :] * apply(vecs[2])
    pair[4:5, :] = row
    psum[pl.ds(chunk_row, 1), :] = row
    send_two_planes(X_S, pair.at[pl.ds(4, 1)], psum, chunk_row)

    where = [ppos[pl.ds(c, 64, stride=4), :] for c in range(4)]

    @pl.loop(0, A)
    def _(i):
        at = [own_at[c, pl.ds(i, 1), :] for c in range(4)]
        dx, dy, dz = (at[c] - where[c] for c in range(3))
        r2 = jnp.maximum(dx * dx + dy * dy + dz * dz, 1.0)
        value, peak, inverse = smeared(r2, at[3] + where[3])
        slope = inverse * inverse * (peak - value)
        for v in range(2):
            weight = slope * vecs[3 - v]
            mx, my, mz = weight * dx, weight * dy, weight * dz
            outs = (mx, my, mz, mx * dx, my * dy, mz * dz, mx * dy, mx * dz, my * dz)
            for c, terms in enumerate(outs):
                rows9[v, c, pl.ds(i, 1), :] = jnp.sum(terms, axis=0, keepdims=True)

    sums = [
        [to_row(jnp.sum(rows9[v, c], axis=1, keepdims=True)) for c in range(9)] for v in range(2)
    ]
    own_row = 2 * s + half
    await_rows(recv_sem.at[X_S], psum, 2 * NS - 1)
    second_alpha = fresh / total(psum[...])
    charge = vecs[3, pl.ds(own_row, 1), :] + second_alpha * vecs[2, pl.ds(own_row, 1), :]
    moment = [sums[0][c] + second_alpha * sums[1][c] for c in range(9)]
    result = []
    for c in range(3):
        force = -charge * moment[c]
        result.append(force + charge * field[0] if c == 2 else force)
    result.append(charge)
    result.append(jnp.zeros((4, L), f32))
    for c in range(3, 9):
        result.append(0.5 * charge * moment[c])
    result.append(jnp.zeros((2, L), f32))
    result = jnp.concatenate(result, axis=0)
    result = pltpu.roll(result, lax.rem(L - off, L), axis=1)
    q_out[...] = result[3:4, 0:A]
    f_out[...] = result[0:3, 0:A]
    v_out[...] = result[8:14, 0:A]

    for which, dst, rows in (
        (X_LIST, list_in, NS - 1),
        (X_FEAT, feat_in, (NS - 1) * A),
        (X_POS_Z, zpos, (NZ - 1) * 8),
        (X_POS_P + own_group, ppos, (NS - 1) * 8),
        (X_B_Z, zvec, NZ - 1),
        (X_B_P, vecs.at[0], (NS - 1) * 2),
        (X_Y, vecs.at[1], 2 * NS - 1),
        (X_S, psum, 2 * NS - 1),
    ):
        await_rows(send_sem.at[which], dst, rows)


def hand_out(*refs):
    copies = [pltpu.make_async_copy(refs[k], refs[4 + k], refs[8].at[k]) for k in range(4)]
    for copy in copies:
        copy.start()
    for copy in copies:
        copy.wait()


def shards(*given):
    given = list(given)
    for k, shape in ((2, (1, A)), (4, (1, E)), (5, (1, E)), (11, (1, L))):
        given[k] = given[k].reshape(shape)
    vmem = pl.BlockSpec(memory_space=pltpu.VMEM)
    hbm = pl.BlockSpec(memory_space=pltpu.HBM)
    held = [pltpu.VMEM(x.shape, x.dtype) for x in given[:12]]
    held += [pltpu.SMEM(x.shape, x.dtype) for x in given[12:]]
    results = (
        jax.ShapeDtypeStruct((A, L), bf16),
        jax.ShapeDtypeStruct((1, A), f32),
        jax.ShapeDtypeStruct((3, A), f32),
        jax.ShapeDtypeStruct((6, A), f32),
    )
    made = pl.pallas_call(
        kernel,
        out_shape=results,
        in_specs=[hbm] * 16,
        out_specs=[vmem] * 4,
        scratch_shapes=held
        + [
            pltpu.VMEM((NS, L), jnp.int32),
            pltpu.VMEM((L, L), jnp.int32),
            pltpu.VMEM((NS * A, L), bf16),
            pltpu.VMEM((8, L), f32),
            pltpu.VMEM((8, L), f32),
            pltpu.VMEM((NZ * 8, L), f32),
            pltpu.VMEM((16, L), f32),
            pltpu.VMEM((NS * 8, L), f32),
            pltpu.VMEM((NZ, L), f32),
            pltpu.VMEM((8, L), f32),
            pltpu.VMEM((4, 2 * NS, L), f32),
            pltpu.VMEM((2 * NS, L), f32),
            pltpu.VMEM((E, 4 * L), f32),
            pltpu.VMEM((E, L), f32),
            pltpu.VMEM((E, L), f32),
            pltpu.VMEM((E, L), bf16),
            pltpu.VMEM((8, E), f32),
            pltpu.VMEM((4, L, L), f32),
            pltpu.VMEM((4, A, L), f32),
            pltpu.VMEM((L, 2 * NS, L), f32),
            pltpu.VMEM((8 * L, L), f32),
            pltpu.VMEM((2, 9, A, L), f32),
            pltpu.SemaphoreType.DMA((EXCHANGES,)),
            pltpu.SemaphoreType.DMA((EXCHANGES,)),
            pltpu.SemaphoreType.DMA((16,)),
            pltpu.SemaphoreType.REGULAR,
            pltpu.SemaphoreType.REGULAR,
        ],
        compiler_params=pltpu.CompilerParams(
            collective_id=0, has_side_effects=True, vmem_limit_bytes=60 * 1024 * 1024
        ),
    )(*given)
    new_features, charges, forces, virial = pl.pallas_call(
        hand_out,
        out_shape=results,
        in_specs=[hbm] * 4,
        out_specs=[hbm] * 4,
        scratch_shapes=[pltpu.SemaphoreType.DMA((4,))],
    )(*made)
    return new_features, charges.reshape(A), forces, virial


def solution(mesh):
    atoms = P(("row", "space"))
    columns = P(None, ("row", "space"))
    return jax.shard_map(
        shards,
        mesh=mesh,
        in_specs=(
            P(("row", "space"), None), columns, atoms, P("row", "space", None), atoms, atoms, columns,
        )
        + (P(),) * 9,
        out_specs=(P(("row", "space"), None), atoms, columns, columns),
        check_vma=False,
    )
```

```python
import functools
import math

import jax
import jax.numpy as jnp
from jax import lax
from jax.experimental import pallas as pl
from jax.experimental.pallas import tpu as pltpu
from jax.sharding import PartitionSpec as P

MESH = pl.DeviceIdType.MESH
NZ = 16
NS = 32
A = 16
L = 128
E = 512

CUTOFF = 6.0
MESSAGE_SCALE = 0.125
TWO_OVER_ROOT_PI = 2.0 / math.sqrt(math.pi)
LOG2E = math.log2(math.e)
INVERSE_ROOT_PI = 1.0 / math.sqrt(math.pi)

ERF_P = 0.55
ERF_C = (0.30158329, 0.39084308, -0.04142873, 0.75971775, -0.51804038, 0.10732501)

X_LIST, X_FEAT, X_POS_Z, X_B_Z, X_B_P, X_Y, X_S, X_POS_P = range(8)
GROUPS = 8
EXCHANGES = X_POS_P + GROUPS
GROUP_ORDER = (0, 2, 6, 1, 4, 3, 7, 5)
EARLY = 1


def hops(k):
    return (0, 1, 2, 1)[k // 8] + (0, 1, 2, 1)[k // 2 % 4] + 0.3 * (k % 2)


PEERS = sorted(range(1, NS), key=hops, reverse=True)
PAIR_PEERS = sorted(
    [(other, k) for other in (0, 1) for k in range(NS) if other or k],
    key=lambda at: at[0] + hops(at[1]),
    reverse=True,
)

f32 = jnp.float32
bf16 = jnp.bfloat16


def iota(shape, dim):
    return lax.broadcasted_iota(jnp.int32, shape, dim)


def reciprocal(x):
    guess = pl.reciprocal(x, approx=True)
    return guess * (2.0 - x * guess)


def smeared(r2, spread):
    inverse = lax.rsqrt(r2)
    scale = lax.rsqrt(spread)
    x = r2 * inverse * scale
    bell = jnp.exp2(-(x * x))
    t = reciprocal(1.0 + (ERF_P / math.sqrt(LOG2E)) * x)
    poly = ERF_C[5]
    for c in ERF_C[4::-1]:
        poly = poly * t + c
    return (1.0 - bell * (poly * t)) * inverse, (TWO_OVER_ROOT_PI / math.sqrt(LOG2E)) * scale * bell, inverse


def kernel(*refs):
    given = refs[:16]
    nf_out, q_out, f_out, v_out = refs[16:20]
    held = refs[20:36]
    (
        lists, list_in, feat_in, own_in, packet, zpos, line, ppos, zvec, pair, vecs, psum,
        fil, base, slot, first, columns, coords, own_at, green, part, rows9,
        send_sem, recv_sem, in_sem, plane_ready, line_ready,
    ) = refs[36:]
    (
        feat, pos, species, ghosts, recv, sender, evec, w_msg, w_rad1, w_rad2, w_up, w_out,
        hardness, width, chi_shift, field,
    ) = held
    z = lax.axis_index("row")
    s = lax.axis_index("space")
    twin = z + 1 - 2 * lax.rem(z, 2)
    barrier = pltpu.get_barrier_semaphore()

    def signal(device):
        pl.semaphore_signal(barrier, inc=1, device_id=device, device_id_type=MESH)

    even = lax.rem(s, 2) == 0
    mate = s + 1 - 2 * lax.rem(s, 2)

    @pl.loop(0, NS // 2)
    def _(k):
        peer = 2 * lax.rem(s // 2 + k, NS // 2)

        @pl.when(peer != s)
        def _():
            signal((z, peer))

    @pl.loop(1, NZ)
    def _(k):
        signal((lax.rem(z + k, NZ), (s // 2) * 2 + 1))

    @pl.when(even)
    def _():
        signal((z, mate))

    def tell(semaphore):
        pl.semaphore_signal(semaphore, inc=1, device_id=(z, mate), device_id_type=MESH)

    loads = [pltpu.make_async_copy(given[k], held[k], in_sem.at[k]) for k in range(16)]
    for load in loads:
        load.start()

    def send(which, source, destination, device):
        pltpu.make_async_remote_copy(
            src_ref=source,
            dst_ref=destination,
            send_sem=send_sem.at[which],
            recv_sem=recv_sem.at[which],
            device_id=device,
            device_id_type=MESH,
        ).start()

    def send_z(which, src, dst, rows):
        to = dst.at[pl.ds(z * rows, rows)]
        send(which, src, to, (lax.rem(z + 8, NZ), s))

        @pl.loop(1, 8)
        def _(k):
            send(which, src, to, (lax.rem(z + 8 - k, NZ), s))
            send(which, src, to, (lax.rem(z + 8 + k, NZ), s))

    def send_p(which, source, dst, rows):
        at = pl.multiple_of(s * rows, rows)
        for k in PEERS:
            send(which, source(s ^ k), dst.at[pl.ds(at, rows)], (z, s ^ k))

    def send_two_planes(which, src, dst, at):
        for other, k in PAIR_PEERS:
            send(which, src, dst.at[pl.ds(at, 1)], (twin if other else z, s ^ k))

    def await_rows(sem, dst, rows):
        some = dst.at[pl.ds(0, rows)]
        pltpu.make_async_copy(some, some, sem).wait()

    lane = iota((1, L), 1)
    half = z // 8
    off = lax.rem(z, 8) * A
    mine = (lane >= off) & (lane < off + A)
    diagonal = iota((A, L), 1) == iota((A, L), 0) + off
    chunk = lax.rem(z, 2)

    def to_row(column):
        return jnp.sum(jnp.where(diagonal, column, 0.0), axis=0, keepdims=True)

    for load in loads:
        load.wait()
    own_in[...] = jnp.zeros_like(own_in)
    own_in[0:3, 0:A] = pos[...]
    own_in[3:4, 0:A] = species[...].astype(f32)
    own = pltpu.roll(own_in[...], off, axis=1)
    kind = own[3:4]

    def lookup(table):
        out = jnp.zeros((1, L), f32)
        for k in range(4):
            out = out + jnp.where(mine & (kind == k), table[k], 0.0)
        return out

    sigma = jnp.where(mine, lookup(width), 1.0)
    spread = jnp.where(mine, (2.0 / LOG2E) * sigma * sigma, 0.0)
    packet[0:3, :] = own[0:3]
    packet[3:4, :] = spread
    packet[4:5, :] = jnp.where(mine, lookup(hardness) + INVERSE_ROOT_PI / sigma, 0.0)
    packet[5:8, :] = jnp.zeros((3, L), f32)
    back = pltpu.roll(packet[...], lax.rem(L - off, L), axis=1)
    folded = back[0:1]
    for c in range(1, 5):
        folded = folded + pltpu.roll(back[c : c + 1], A * c, axis=1)
    line[12:13, :] = folded
    for c in range(4):
        column = jnp.sum(jnp.where(diagonal, packet[c : c + 1, :], 0.0), axis=1, keepdims=True)
        own_at[c] = jnp.broadcast_to(column, (A, L))
    lists[...] = jnp.zeros_like(lists)
    lists[:, 0:NS] = ghosts[0]
    list_in[NS:, :] = jnp.zeros((L - NS, L), jnp.int32)

    vectors = evec[...]
    squared = vectors[0:1] * vectors[0:1] + vectors[1:2] * vectors[1:2] + vectors[2:3] * vectors[2:3]
    length = jnp.sqrt(squared)
    unit = vectors / length
    ratio = length / CUTOFF
    envelope = (1.0 - ratio * ratio) * (1.0 - ratio * ratio)
    order = (iota((8, 1), 0) + 1).astype(f32)
    basis = jnp.sin(order * math.pi * ratio) / ratio * envelope
    mixed = lax.dot_general(
        basis, w_rad1[...], (((0,), (0,)), ((), ())),
        precision=lax.Precision.HIGHEST, preferred_element_type=f32,
    )
    radial = jax.nn.silu(mixed).astype(bf16)
    filters = jnp.dot(radial, w_rad2[...], preferred_element_type=f32)
    slots = sender[...]
    local = slots < A
    ghost = slots - A
    columns[0:3, :] = unit
    columns[3:4, :] = jnp.where(local, s * A + slots, (ghost // NS) * A).astype(f32)
    columns[4:5, :] = jnp.where(local, -1, ghost // NS).astype(f32)
    columns[5:6, :] = lax.rem(jnp.where(local, 0, ghost), NS).astype(f32)
    columns[6:8, :] = jnp.zeros((2, E), f32)

    @pl.when(even)
    def _():
        pl.semaphore_wait(barrier, NS - 1)
        tell(plane_ready)

    @pl.when(jnp.logical_not(even))
    def _():
        pl.semaphore_wait(plane_ready, 1)

    feat_at = pl.multiple_of(s * A, A)
    for k in PEERS:
        peer = s ^ k
        send(X_LIST, lists.at[pl.ds(peer, 1)], list_in.at[pl.ds(s, 1)], (z, peer))
        send(X_FEAT, feat, feat_in.at[pl.ds(feat_at, A)], (z, peer))
    turned = columns[...].T
    fil[:, 0:L] = filters[:, 0:L]
    for c in range(3):
        fil[:, (c + 1) * L : (c + 2) * L] = filters[:, L:] * turned[:, c : c + 1]
    lane_f = iota((E, L), 1).astype(f32)
    base[...] = lane_f - turned[:, 3:4]
    first[...] = jnp.where(lane_f == turned[:, 4:5], 1.0, 0.0).astype(bf16)
    slot[...] = jnp.where(lane_f == turned[:, 5:6], 1.0, 0.0)
    receivers = jnp.where(iota((A, E), 0) == recv[...], 1.0, 0.0).astype(bf16)

    @pl.when(even)
    def _():
        pl.semaphore_wait(line_ready, 1)

    @pl.when(jnp.logical_not(even))
    def _():
        pl.semaphore_wait(barrier, 2 * NZ - 1)
        tell(line_ready)

    send_z(X_POS_Z, line.at[pl.ds(12, 1)], zpos, 1)
    list_in[pl.ds(s, 1), :] = lists[pl.ds(s, 1), :]
    feat_in[pl.ds(feat_at, A), :] = feat[...]
    zpos[pl.ds(z, 1), :] = line[12:13, :]

    await_rows(recv_sem.at[X_LIST], list_in, NS - 1)
    found = jnp.dot(first[...], list_in[...].astype(f32).astype(bf16), preferred_element_type=f32)
    found = (found * slot[...]).astype(bf16)
    found = jnp.dot(found, jnp.ones((L, L), bf16), preferred_element_type=f32)
    offset = base[...] - found
    picks = jnp.concatenate(
        [jnp.where(offset == float(-L * g), 1.0, 0.0).astype(bf16) for g in range(4)], axis=1
    )
    await_rows(recv_sem.at[X_FEAT], feat_in, (NS - 1) * A)
    table = jnp.dot(feat_in[...], w_msg[...], preferred_element_type=f32).astype(bf16)
    projected = jnp.dot(picks, table, preferred_element_type=f32)
    lower, upper = projected[:, 0:L], projected[:, L:]
    message = jnp.concatenate(
        [(lower * fil[:, 0:L]).astype(bf16)]
        + [(upper * fil[:, (c + 1) * L : (c + 2) * L]).astype(bf16) for c in range(3)],
        axis=1,
    )
    summed = jnp.dot(receivers, message, preferred_element_type=f32) * MESSAGE_SCALE
    norms = summed[:, L : 2 * L] * summed[:, L : 2 * L]
    for c in range(2, 4):
        norms = norms + summed[:, c * L : (c + 1) * L] * summed[:, c * L : (c + 1) * L]
    invariant = jnp.concatenate([summed[:, 0:L], norms], axis=1).astype(bf16)
    hidden = jax.nn.silu(jnp.dot(invariant, w_up[...], preferred_element_type=f32))
    nf_out[...] = (feat[...].astype(f32) + hidden).astype(bf16)
    chi = to_row(jnp.sum(hidden * w_out[...], axis=1, keepdims=True)) + lookup(chi_shift)
    rhs = jnp.where(mine, field[0] * own[2:3] - chi, 0.0)

    pair[2:3, :] = rhs
    zvec[pl.ds(z, 1), :] = rhs
    send_z(X_B_Z, pair.at[pl.ds(2, 1)], zvec, 1)

    await_rows(recv_sem.at[X_POS_Z], zpos, NZ - 1)
    tall, wide = iota((8, L), 0), iota((8, L), 1) // A
    masks = [(tall == r) & (wide == r) for r in range(8)]
    for h in range(2):
        tile = zpos[8 * h : 8 * h + 8, :]
        shifted = [tile] + [pltpu.roll(tile, A * d, axis=1) for d in range(1, 8)]
        for c in range(5):
            terms = [jnp.where(masks[r], shifted[(r - c) % 8], 0.0) for r in range(8)]
            while len(terms) > 1:
                terms = [a + b for a, b in zip(terms[::2], terms[1::2])]
            at_line = h * 4 + c if c < 4 else 8 + h
            line[at_line : at_line + 1, :] = jnp.sum(terms[0], axis=0, keepdims=True)
    own_group = s // 4

    send_p(X_POS_P + own_group, lambda peer: line.at[pl.ds(0, 8)], ppos, 8)
    ppos[pl.ds(pl.multiple_of(s * 8, 8), 8), :] = line[0:8, :]
    for c in range(4):
        spread_out = jnp.broadcast_to(line[pl.ds(chunk * 4 + c, 1), :], (L, L))
        coords[c] = spread_out.T
    diag_row = line[pl.ds(8 + chunk, 1), :]
    own_at_row = lax.rem(2 * s + chunk, 8)

    def fill(turn):
        group = own_group ^ GROUP_ORDER[turn]
        await_rows(recv_sem.at[X_POS_P + group], ppos, (3 if turn == 0 else 4) * 8)
        xs = [ppos[pl.ds(group * 32 + c, 8, stride=4), :] for c in range(4)]
        at_row = pl.multiple_of(group * 8, 8)

        @pl.loop(0, L, step=8)
        def _(i0):
            for i in range(8):
                at = [coords[c, pl.ds(i0 + i, 1), :] for c in range(4)]
                dx, dy, dz = (at[c] - xs[c] for c in range(3))
                r2 = dx * dx + dy * dy + dz * dz
                if turn == 0:
                    r2 = jnp.maximum(r2, 1.0)
                value = smeared(r2, at[3] + xs[3])[0]
                if turn == 0:
                    itself = (iota((8, L), 0) == own_at_row) & (iota((8, L), 1) == i0 + i)
                    value = jnp.where(itself, diag_row, value)
                green[i0 + i, pl.ds(at_row, 8), :] = value

    for turn in range(EARLY):
        fill(turn)
    await_rows(recv_sem.at[X_B_Z], zvec, NZ - 1)
    low = jnp.sum(zvec[0:8, :], axis=0, keepdims=True)
    high = jnp.sum(zvec[8:16, :], axis=0, keepdims=True)
    pair[0:1, :] = low
    pair[1:2, :] = high
    send_p(X_B_P, lambda peer: pair.at[pl.ds(0, 2)], vecs.at[0], 2)
    vecs[0, pl.ds(2 * s, 1), :] = low
    vecs[0, pl.ds(2 * s + 1, 1), :] = high
    for turn in range(EARLY, GROUPS):
        fill(turn)

    chunk_row = 2 * s + chunk

    def apply(vector):
        @pl.loop(0, L, step=4)
        def _(i0):
            for i in range(4):
                terms = [
                    green[i0 + i, 8 * g : 8 * g + 8, :] * vector[8 * g : 8 * g + 8]
                    for g in range(GROUPS)
                ]
                while len(terms) > 1:
                    terms = [a + b for a, b in zip(terms[::2], terms[1::2])]
                part[pl.ds(pl.multiple_of((i0 + i) * 8, 8), 8), :] = terms[0]

        rows = [part[pl.ds(k, L, stride=8), :] for k in range(8)]
        while len(rows) > 1:
            rows = [a + b for a, b in zip(rows[::2], rows[1::2])]
        return jnp.sum(rows[0].T, axis=0, keepdims=True)

    def total(value):
        return jnp.sum(jnp.sum(value, axis=0, keepdims=True), axis=1, keepdims=True)

    await_rows(recv_sem.at[X_B_P], vecs.at[0], (NS - 1) * 2)
    rhs_all = vecs[0]
    image = apply(rhs_all)
    pair[3:4, :] = image
    vecs[1, pl.ds(chunk_row, 1), :] = image
    send_two_planes(X_Y, pair.at[pl.ds(3, 1)], vecs.at[1], chunk_row)
    norm = total(rhs_all * rhs_all)
    await_rows(recv_sem.at[X_Y], vecs.at[1], 2 * NS - 1)
    image_all = vecs[1]
    alpha = norm / total(rhs_all * image_all)
    residual = rhs_all - alpha * image_all
    fresh = total(residual * residual)
    beta = fresh / norm
    vecs[2] = residual + beta * rhs_all
    vecs[3] = alpha * rhs_all
    row = vecs[2, pl.ds(chunk_row, 1), :] * apply(vecs[2])
    pair[4:5, :] = row
    psum[pl.ds(chunk_row, 1), :] = row
    send_two_planes(X_S, pair.at[pl.ds(4, 1)], psum, chunk_row)

    where = [ppos[pl.ds(c, 64, stride=4), :] for c in range(4)]

    @pl.loop(0, A)
    def _(i):
        at = [own_at[c, pl.ds(i, 1), :] for c in range(4)]
        dx, dy, dz = (at[c] - where[c] for c in range(3))
        r2 = jnp.maximum(dx * dx + dy * dy + dz * dz, 1.0)
        value, peak, inverse = smeared(r2, at[3] + where[3])
        slope = inverse * inverse * (peak - value)
        for v in range(2):
            weight = slope * vecs[3 - v]
            mx, my, mz = weight * dx, weight * dy, weight * dz
            outs = (mx, my, mz, mx * dx, my * dy, mz * dz, mx * dy, mx * dz, my * dz)
            for c, terms in enumerate(outs):
                rows9[v, c, pl.ds(i, 1), :] = jnp.sum(terms, axis=0, keepdims=True)

    sums = [
        [to_row(jnp.sum(rows9[v, c], axis=1, keepdims=True)) for c in range(9)] for v in range(2)
    ]
    own_row = 2 * s + half
    await_rows(recv_sem.at[X_S], psum, 2 * NS - 1)
    second_alpha = fresh / total(psum[...])
    charge = vecs[3, pl.ds(own_row, 1), :] + second_alpha * vecs[2, pl.ds(own_row, 1), :]
    moment = [sums[0][c] + second_alpha * sums[1][c] for c in range(9)]
    result = []
    for c in range(3):
        force = -charge * moment[c]
        result.append(force + charge * field[0] if c == 2 else force)
    result.append(charge)
    result.append(jnp.zeros((4, L), f32))
    for c in range(3, 9):
        result.append(0.5 * charge * moment[c])
    result.append(jnp.zeros((2, L), f32))
    result = jnp.concatenate(result, axis=0)
    result = pltpu.roll(result, lax.rem(L - off, L), axis=1)
    q_out[...] = result[3:4, 0:A]
    f_out[...] = result[0:3, 0:A]
    v_out[...] = result[8:14, 0:A]

    for which, dst, rows in (
        (X_LIST, list_in, NS - 1),
        (X_FEAT, feat_in, (NS - 1) * A),
        (X_POS_Z, zpos, NZ - 1),
        (X_POS_P + own_group, ppos, (NS - 1) * 8),
        (X_B_Z, zvec, NZ - 1),
        (X_B_P, vecs.at[0], (NS - 1) * 2),
        (X_Y, vecs.at[1], 2 * NS - 1),
        (X_S, psum, 2 * NS - 1),
    ):
        await_rows(send_sem.at[which], dst, rows)


def hand_out(*refs):
    copies = [pltpu.make_async_copy(refs[k], refs[4 + k], refs[8].at[k]) for k in range(4)]
    for copy in copies:
        copy.start()
    for copy in copies:
        copy.wait()


def shards(*given):
    given = list(given)
    for k, shape in ((2, (1, A)), (4, (1, E)), (5, (1, E)), (11, (1, L))):
        given[k] = given[k].reshape(shape)
    vmem = pl.BlockSpec(memory_space=pltpu.VMEM)
    hbm = pl.BlockSpec(memory_space=pltpu.HBM)
    held = [pltpu.VMEM(x.shape, x.dtype) for x in given[:12]]
    held += [pltpu.SMEM(x.shape, x.dtype) for x in given[12:]]
    results = (
        jax.ShapeDtypeStruct((A, L), bf16),
        jax.ShapeDtypeStruct((1, A), f32),
        jax.ShapeDtypeStruct((3, A), f32),
        jax.ShapeDtypeStruct((6, A), f32),
    )
    made = pl.pallas_call(
        kernel,
        out_shape=results,
        in_specs=[hbm] * 16,
        out_specs=[vmem] * 4,
        scratch_shapes=held
        + [
            pltpu.VMEM((NS, L), jnp.int32),
            pltpu.VMEM((L, L), jnp.int32),
            pltpu.VMEM((NS * A, L), bf16),
            pltpu.VMEM((8, L), f32),
            pltpu.VMEM((8, L), f32),
            pltpu.VMEM((NZ, L), f32),
            pltpu.VMEM((16, L), f32),
            pltpu.VMEM((NS * 8, L), f32),
            pltpu.VMEM((NZ, L), f32),
            pltpu.VMEM((8, L), f32),
            pltpu.VMEM((4, 2 * NS, L), f32),
            pltpu.VMEM((2 * NS, L), f32),
            pltpu.VMEM((E, 4 * L), f32),
            pltpu.VMEM((E, L), f32),
            pltpu.VMEM((E, L), f32),
            pltpu.VMEM((E, L), bf16),
            pltpu.VMEM((8, E), f32),
            pltpu.VMEM((4, L, L), f32),
            pltpu.VMEM((4, A, L), f32),
            pltpu.VMEM((L, 2 * NS, L), f32),
            pltpu.VMEM((8 * L, L), f32),
            pltpu.VMEM((2, 9, A, L), f32),
            pltpu.SemaphoreType.DMA((EXCHANGES,)),
            pltpu.SemaphoreType.DMA((EXCHANGES,)),
            pltpu.SemaphoreType.DMA((16,)),
            pltpu.SemaphoreType.REGULAR,
            pltpu.SemaphoreType.REGULAR,
        ],
        compiler_params=pltpu.CompilerParams(
            collective_id=0, has_side_effects=True, vmem_limit_bytes=60 * 1024 * 1024
        ),
    )(*given)
    new_features, charges, forces, virial = pl.pallas_call(
        hand_out,
        out_shape=results,
        in_specs=[hbm] * 4,
        out_specs=[hbm] * 4,
        scratch_shapes=[pltpu.SemaphoreType.DMA((4,))],
    )(*made)
    return new_features, charges.reshape(A), forces, virial


def solution(mesh):
    atoms = P(("row", "space"))
    columns = P(None, ("row", "space"))
    return jax.shard_map(
        shards,
        mesh=mesh,
        in_specs=(
            P(("row", "space"), None), columns, atoms, P("row", "space", None), atoms, atoms, columns,
        )
        + (P(),) * 9,
        out_specs=(P(("row", "space"), None), atoms, columns, columns),
        check_vma=False,
    )
```
